32 devices in a mesh: groups: 2 (over y), dp: 4 (over x, core), tensor: 4 (over z).
Axes of the slice: x: 2, y: 2, z: 4, core: 2. Of those that a mesh axis runs over, the one named last changes fastest.
Arguments:
- tokens: bfloat16 [4096, 8192], P(('groups', 'dp'), 'tensor'), parts along dimension 0, may hold values from -6 to 6
- weight: bfloat16 [8192, 8192], P('tensor'), may hold values from -0.09375 to 0.09375
- down_weight_stack: bfloat16 [64, 64, 8192], P('dp', None, 'tensor'), may hold values from -0.0625 to 0.0625
- up_weight_stack: bfloat16 [64, 64, 8192], P('dp', None, 'tensor'), may hold values from -0.75 to 0.75
- fetch_list: int32 [8, 4, 8], P(('groups', 'dp')), parts along dimension 0, may hold values from 0 to 15, as said below
- choose: int32 [4096], P(('groups', 'dp')), parts along dimension 0, may hold values from 0 to 31
Outputs:
- mixed: bfloat16 [4096, 8192], P(('groups', 'dp'), 'tensor'), parts along dimension 0
The draws below stay inside these ranges and needn't reach their ends.
There are 2 independent parts, one for each index of `groups`. The reference program is written for one: setup_inputs(seed, part) draws one part's arguments, and reference() takes and returns one part's arrays. A program takes and returns all parts, laid end to end along the dimension named above; an argument that names none is the same for every part. Nothing has to cross between parts.
Inputs may be any that keep to these rules, and one draw needn't show every extreme that they name: fetch_list[d, j] holds 8 different slots of owner j.
All inputs are finite; a program needn't handle non-finite values.
Results may differ from the reference program's by a relative error of at most 0.0025.
Values may be sent and summed in bfloat16 or wider, within the bound.
No kernel may reach another device: no remote copies, remote signals or barrier semaphores. Data moves between devices by JAX's collectives and lax.ppermute only.
A program may use at most 192 MiB of HBM per device.

```python
import math
import jax
import jax.numpy as jnp
import numpy as np
from jax import lax

D = 8192
RANK = 64
ADP_DEV = 16
K_PER = 8
ROWS = 2048
ADAPTERS = 64
N_DP = 4


def draw_fetch_list(key, part):
    key = jax.random.fold_in(key, 7)
    keys = jax.random.split(key, N_DP * N_DP)
    orders = jax.vmap(lambda one: jax.random.permutation(one, ADP_DEV))(keys)
    return orders[:, :K_PER].reshape(N_DP, N_DP, K_PER).astype(jnp.int32)


def touch_ends(drawn, stream_key, low, high):
    longest = drawn.shape.index(max(drawn.shape))
    spots = []
    for shift in (0, 1):
        where = [jax.random.randint(jax.random.fold_in(stream_key, axis), (), 0, length) for axis, length in enumerate(drawn.shape)]
        where[longest] = (where[longest] + shift) % drawn.shape[longest]
        spots.append(tuple(where))
    return drawn.at[spots[0]].set(low).at[spots[1]].set(high)


def strengthened(values, rng, source, target, blocks, factor):
    def block_of(dim):
        return (jnp.arange(values.shape[dim]) // (values.shape[dim] // blocks)).reshape((-1,) + (1,) * (values.ndim - 1 - dim))

    first = jax.random.permutation(rng, blocks)[block_of(target)]
    far = (block_of(target) + blocks // 2) % blocks
    return jnp.where((block_of(source) == first) | (block_of(source) == far), factor * values, values)


def level_of(rng, dims, pieces, low, high):
    def one(position, blocks):
        draws = jax.random.uniform(jax.random.fold_in(jax.random.fold_in(rng, 6), position), (blocks,), jnp.float32, low / len(pieces), high / len(pieces))
        return jnp.repeat(jnp.exp(draws), dims[position] // blocks).reshape((-1,) + (1,) * (len(dims) - position - 1))

    loudness = one(*pieces[0])
    for cut in pieces[1:]:
        loudness = loudness * one(*cut)
    return loudness


def rank_bounds(count, lean):
    portions = [(1 << 20) // math.isqrt(rank ** lean) + 1 for rank in range(1, count + 1)]
    spread = 1 + sum(portions) // (1 << 30)
    return np.cumsum(np.array([max(1, weight // spread) for weight in portions]))


def skewed_ids(key, shape, amount, lean):
    grid = rank_bounds(amount, lean)
    lot = jax.random.randint(jax.random.fold_in(key, 1), shape, 0, int(grid[amount - 1]))
    rank = jnp.searchsorted(jnp.asarray(grid, jnp.int32), lot, side="right")
    return jax.random.permutation(jax.random.fold_in(key, 2), amount)[rank].astype(jnp.int32)


def scatter_about(rng, dims, width, bound, shards=(), kind=jnp.bfloat16):
    array = jax.random.normal(rng, dims, jnp.float32) * width
    if len(shards) > 0:
        array = level_of(rng, dims, shards, -0.22, 0.18) * array
    return jnp.clip(array, min=-bound, max=bound).astype(kind)


def heavy_noise(stream_key, extent, deviation, most, pieces, heavy, held_as=jnp.bfloat16):
    values = deviation * jax.random.normal(stream_key, extent, jnp.float32)
    if pieces:
        values = values * level_of(stream_key, extent, pieces, -0.22, 0.18)
    return jnp.clip(strengthened(values, jax.random.fold_in(stream_key, 3), *heavy), -most, most).astype(held_as)


def setup_inputs(seed: int = 0, part: int = 0) -> dict:
    key_of = jax.random.split(jax.random.key(seed), 7)
    part_splits = jax.random.split(jax.random.fold_in(key_of[6], part), 7)
    return {
        "tokens": scatter_about(part_splits[0], (ROWS, D), 1.0, 6.0, ((0, 4), (1, 4))),
        "weight": heavy_noise(key_of[1], (D, D), D ** -0.5, 0.09375, ((0, 4),), (0, 1, 4, 2.0)),
        "down_weight_stack": scatter_about(key_of[2], (ADAPTERS, RANK, D), D ** -0.5, 0.0625, ((0, 4), (2, 4))),
        "up_weight_stack": scatter_about(key_of[3], (ADAPTERS, RANK, D), RANK ** -0.5, 0.75, ((0, 4), (2, 4))),
        "fetch_list": draw_fetch_list(jax.random.fold_in(jax.random.fold_in(key_of[6], part), 71), part),
        "choose": touch_ends(skewed_ids(part_splits[5], (ROWS,), N_DP * K_PER, 2), jax.random.fold_in(part_splits[5], 3), 0, (N_DP * K_PER) - 1).astype(jnp.int32),
    }


adapter_scale = 0.5


def reference(tokens, weight, down_weight_stack, up_weight_stack, fetch_list, choose):
    owners = fetch_list.shape[0]
    per_owner = fetch_list.shape[2]
    fetched_weights = owners * per_owner
    adapter_rank = down_weight_stack.shape[1]
    hidden_width = down_weight_stack.shape[2]
    adp = down_weight_stack.shape[0] // owners
    token_row_count = tokens.shape[0] // owners
    token_blocks = tokens.reshape(owners, token_row_count, hidden_width)
    choose_blocks = choose.reshape(owners, token_row_count)

    def one_block(packed):
        row_block, wanted, picks = packed
        adapter_slot_index = (jnp.arange(owners, dtype=jnp.int32)[:, None] * adp + wanted).reshape(-1).astype(jnp.int32)
        down_weight_picked = down_weight_stack[adapter_slot_index].reshape(fetched_weights * adapter_rank, hidden_width)
        up_weight_picked = up_weight_stack[adapter_slot_index].reshape(fetched_weights * adapter_rank, hidden_width)
        base_output_part = jnp.dot(row_block, weight, preferred_element_type=jnp.float32)
        partial_sums = lax.dot_general(row_block, down_weight_picked, (((1,), (1,)), ((), ())), preferred_element_type=jnp.float32)
        partial_sums = partial_sums.reshape(token_row_count, fetched_weights, adapter_rank)
        shrink = jnp.take_along_axis(partial_sums, picks[:, None, None].astype(jnp.int32), axis=1)[:, 0, :]
        low_rank_shrink = shrink.astype(jnp.bfloat16)
        adapter_selector = (picks[:, None] == jnp.arange(fetched_weights, dtype=jnp.int32)[None, :]).astype(jnp.bfloat16)
        spread_output = (low_rank_shrink[:, None, :] * adapter_selector[:, :, None]).reshape(token_row_count, fetched_weights * adapter_rank)
        adapted_output = jnp.dot(spread_output, up_weight_picked, preferred_element_type=jnp.float32)
        return (base_output_part + adapter_scale * adapted_output).astype(jnp.bfloat16)

    result = lax.map(one_block, (token_blocks, fetch_list, choose_blocks))
    return result.reshape(owners * token_row_count, hidden_width)
```

```python
import functools

import jax
import jax.numpy as jnp
from jax import lax
from jax.experimental import pallas as pl
from jax.experimental.pallas import tpu as pltpu
from jax.sharding import PartitionSpec as P

adapter_scale = 0.5
CORES = 2
PIECES = 2
BANK_PIECES = 2
BASE_WIRE = 8.0
LOW_WIRE = 0.5
VMEM = 48 * 1024 * 1024


def after(value, *others):
    return lax.optimization_barrier((value, *others))[0]


def ids_of_pair(ids_ref, first, shape, rank):
    lane = lax.broadcasted_iota(jnp.int32, shape, 1)
    return jnp.where(lane < rank, ids_ref[first], ids_ref[first + 1])


def shrink_kernel(rank, ids_ref, g_ref, tokens_ref, *refs):
    *blocks, o_ref = refs
    tokens = tokens_ref[...]
    g = g_ref[...]
    total = jnp.zeros(o_ref.shape, jnp.float32)
    seen = 0
    for block in blocks:
        part = lax.dot_general(tokens, block[...], (((1,), (1,)), ((), ())), preferred_element_type=jnp.float32)
        for pair in range(block.shape[0] // (2 * rank)):
            ids = ids_of_pair(ids_ref, seen + 2 * pair, o_ref.shape, rank)
            total += jnp.where(g == ids, part[:, pair * 2 * rank : (pair + 1) * 2 * rank], 0.0)
        seen += block.shape[0] // rank
    o_ref[...] = total


def expand_kernel(rank, has_base, ids_ref, g_ref, low_ref, *refs):
    *blocks, o_ref = refs
    base = None
    if has_base:
        base, *blocks = blocks
    g = g_ref[...]
    low = low_ref[...].astype(jnp.float32)
    total = jnp.zeros(o_ref.shape, jnp.float32)
    seen = 0
    for block in blocks:
        spread = []
        for pair in range(block.shape[0] // (2 * rank)):
            ids = ids_of_pair(ids_ref, seen + 2 * pair, low.shape, rank)
            spread.append(jnp.where(g == ids, low, 0.0).astype(jnp.bfloat16))
        seen += block.shape[0] // rank
        total += jnp.dot(jnp.concatenate(spread, axis=1), block[...], preferred_element_type=jnp.float32)
    total = adapter_scale * total
    o_ref[...] = total if base is None else base[...] + total


def over_rows(kernel, out_width, held, g, ids, rows_in, blocks):
    rows = g.shape[0]
    rank, width = held
    tile = min(256, rows)
    flat = [block.reshape(-1, width) for block in blocks]
    deep = sum(block.shape[0] for block in flat)
    return pl.pallas_call(
        kernel,
        out_shape=jax.ShapeDtypeStruct((rows, out_width), jnp.float32),
        grid_spec=pltpu.PrefetchScalarGridSpec(
            num_scalar_prefetch=1,
            grid=(rows // tile,),
            in_specs=[pl.BlockSpec((tile, 1), lambda i, ids: (i, 0))]
            + [pl.BlockSpec((tile, one.shape[1]), lambda i, ids: (i, 0)) for one in rows_in]
            + [pl.BlockSpec(block.shape, lambda i, ids: (0, 0)) for block in flat],
            out_specs=pl.BlockSpec((tile, out_width), lambda i, ids: (i, 0)),
        ),
        compiler_params=pltpu.CompilerParams(vmem_limit_bytes=VMEM),
        cost_estimate=pl.CostEstimate(
            flops=2 * rows * width * deep,
            bytes_accessed=2 * width * deep + 4 * rows * out_width + sum(one.size * one.dtype.itemsize for one in rows_in),
            transcendentals=0,
        ),
    )(ids, g, *rows_in, *flat)


def along_line(line, z, partial_sums, gates):
    def wire(total):
        return total.astype(jnp.float16)

    def unwire(block):
        return block.astype(jnp.float32)

    def sums(target, piece):
        return BASE_WIRE * partial_sums(target, piece)

    def move(block, pairs):
        return lax.ppermute(block, "tensor", pairs)

    pieces = range(PIECES)
    if line == 4:
        outer = [(0, 1), (3, 2)]
        inner = [(1, 2), (2, 1)]
        both = [(0, 1), (1, 0), (2, 3), (3, 2)]
        low_half = z < 2
        first = jnp.where(low_half, 3, 0)
        second = jnp.where(low_half, 2, 1)
        third = jnp.array([1, 0, 3, 2], jnp.int32)[z]
        sent = []

        def send_out(block, pairs):
            if len(sent) >= 2:
                block = after(block, sent[-2])
            sent.append(move(block, pairs))
            return sent[-1]

        one = [sums(first, p) for p in pieces]
        a1 = [send_out(wire(one[p]), outer) for p in pieces]
        b1 = [move(wire(sums(first, p) + unwire(a1[p])), inner) for p in pieces]
        a2 = [send_out(wire(sums(second, p)), outer) for p in pieces]
        b2 = [move(wire(sums(second, p) + unwire(a2[p])), inner) for p in pieces]
        a3 = [send_out(wire(sums(third, p) + unwire(b1[p])), both) for p in pieces]
        gates.extend(sent)
        return [(unwire(a3[p]) + unwire(b2[p])) * (1.0 / BASE_WIRE) for p in pieces]

    lines = []
    for slot in range(1, line):
        for p in pieces:
            ahead, behind = (z - slot) % line, (z + slot) % line
            if 2 * slot <= line:
                to_right = to_left = sums(jnp.where(z < slot, ahead, behind), p)
            else:
                to_right, to_left = sums(ahead, p), sums(behind, p)
            if slot > 1:
                right, left = lines[-PIECES]
                to_right, to_left = to_right + unwire(right), to_left + unwire(left)
                if 2 * slot <= line:
                    to_right = to_left = to_right + unwire(left)
            going_right = [(i, i + 1) for i in range(slot)]
            going_left = [(line - 1 - i, line - 2 - i) for i in range(slot)]
            lines.append((move(wire(to_right), going_right), move(wire(to_left), going_left)))
    return [(unwire(right) + unwire(left)) * (1.0 / BASE_WIRE) for right, left in lines[-PIECES:]]


def add_and_round(line, z, part):
    rows, rank = part.shape
    packed = jnp.concatenate([part[: rows // 2], part[rows // 2 :]], axis=1)
    size = rows // 2 // line

    def turned(shift):
        return [(i, (i + shift) % line) for i in range(line)]

    def share(i):
        return lax.dynamic_slice(packed, (i * size, 0), (size, 2 * rank))

    total = share(z)
    for shift in range(1, line):
        total = total + lax.ppermute(share((z + shift) % line), "tensor", turned(shift))
    low = total.astype(jnp.bfloat16)
    whole = lax.dynamic_update_slice(jnp.zeros(packed.shape, jnp.bfloat16), low, (z * size, 0))
    for shift in range(1, line):
        other = lax.ppermute(low, "tensor", turned(shift))
        whole = lax.dynamic_update_slice(whole, other, ((z - shift) % line * size, 0))
    return whole


def on_device(tokens, weight, down_stack, up_stack, fetch_list, choose):
    line = lax.axis_size("tensor")
    owners = lax.axis_size("dp")
    groups = lax.axis_size("groups")
    chips = owners // CORES
    z = lax.axis_index("tensor")
    me = lax.axis_index("dp")
    group = lax.axis_index("groups")
    x, core = me // CORES, me % CORES
    own, rank, width = down_stack.shape
    rows = tokens.shape[0]
    per_owner = fetch_list.shape[2]
    sibling = [(i, i ^ 1) for i in range(owners)]
    tiles = rows // PIECES

    def to_sibling(block):
        return lax.ppermute(block, "dp", sibling)

    def partial_sums(target, piece):
        block = lax.dynamic_slice(weight, (0, target * width), (weight.shape[0], width))
        return jnp.dot(tokens[piece * tiles : (piece + 1) * tiles], block, preferred_element_type=jnp.float32)

    gates = []
    arrived = along_line(line, z, partial_sums, gates)

    wanted = (jnp.arange(owners, dtype=jnp.int32)[:, None] * own + fetch_list[0]).reshape(-1)
    picked = choose[:, None] == jnp.arange(owners * per_owner, dtype=jnp.int32)[None, :]
    g = jnp.sum(jnp.where(picked, wanted[None, :], 0), axis=1)

    g_both = jnp.concatenate([g, to_sibling(g)])[:, None]
    tokens_both = jnp.concatenate([tokens, to_sibling(tokens)], axis=0)

    share = own // groups
    size = share // BANK_PIECES

    def slots(owner, first, count):
        return owner * own + first + jnp.arange(count, dtype=jnp.int32)

    found = [[], []]
    crossed, turned = [], []
    for kind, stack in enumerate((down_stack, up_stack)):
        for shift in range(1, chips):
            owner = (x - shift) % chips * CORES + core
            for piece in range(BANK_PIECES):
                first = group * share + piece * size
                block = lax.dynamic_slice(stack, (first, 0, 0), (size, rank, width))
                if crossed:
                    block = after(block, crossed[-1])
                block = lax.ppermute(block, "dp", [(i, (i + shift * CORES) % owners) for i in range(owners)])
                crossed.append(block)
                found[kind].append((block, slots(owner, first, size)))
                for turn in range(1, groups):
                    other = after(block, turned[-1]) if turned else block
                    other = lax.ppermute(other, "groups", [(i, (i + turn) % groups) for i in range(groups)])
                    turned.append(other)
                    first_there = (group - turn) % groups * share + piece * size
                    found[kind].append((other, slots(owner, first_there, size)))

    def shrink(pairs):
        ids = jnp.concatenate([ids for _, ids in pairs])
        kernel = functools.partial(shrink_kernel, rank)
        return over_rows(kernel, 2 * rank, (rank, width), g_both, ids, [tokens_both], [block for block, _ in pairs])

    mine = slots(me, 0, own)
    halves = shrink([(down_stack, mine)]) + shrink(found[0])
    part = halves[:, :rank] + halves[:, rank:]
    part = part[:rows] + to_sibling(part[rows:])
    low = add_and_round(line, z, part)
    low_both = jnp.concatenate([low, to_sibling(low)], axis=1)
    order = [low_both[:, i * rank : (i + 1) * rank] for i in range(4)]
    low_both = jnp.concatenate(order, axis=0)
    low_both = jnp.concatenate([low_both, low_both], axis=1)

    def expand(base, pairs):
        ids = jnp.concatenate([ids for _, ids in pairs])
        kernel = functools.partial(expand_kernel, rank, base is not None)
        rows_in = [low_both] if base is None else [low_both, base]
        return over_rows(kernel, width, (rank, width), g_both, ids, rows_in, [block for block, _ in pairs])

    early, late = found[1][:-1], found[1][-1:]
    adapted = expand(None, [(up_stack, mine)] + early)
    adapted = expand(adapted, late)
    for_sibling = (LOW_WIRE * adapted[rows:]).astype(jnp.float16)
    from_sibling = to_sibling(for_sibling).astype(jnp.float32) * (1.0 / LOW_WIRE)
    outs = []
    for p in range(PIECES):
        here = slice(p * tiles, (p + 1) * tiles)
        outs.append(partial_sums(z, p) + adapted[here] + from_sibling[here] + arrived[p])
    return jnp.concatenate(outs, axis=0).astype(jnp.bfloat16)


def solution(mesh):
    return jax.shard_map(
        on_device,
        mesh=mesh,
        in_specs=(
            P(("groups", "dp"), "tensor"),
            P("tensor", None),
            P("dp", None, "tensor"),
            P("dp", None, "tensor"),
            P(("groups", "dp"), None, None),
            P(("groups", "dp")),
        ),
        out_specs=P(("groups", "dp"), "tensor"),
        check_vma=False,
    )
```

```python
import functools

import jax
import jax.numpy as jnp
from jax import lax
from jax.experimental import pallas as pl
from jax.experimental.pallas import tpu as pltpu
from jax.sharding import PartitionSpec as P

adapter_scale = 0.5
CORES = 2
BANK_PIECES = 2
BASE_WIRE = 8.0
VMEM = 48 * 1024 * 1024


def ids_of_pair(ids_ref, first, shape, rank):
    lane = lax.broadcasted_iota(jnp.int32, shape, 1)
    return jnp.where(lane < rank, ids_ref[first], ids_ref[first + 1])


def shrink_kernel(rank, steps, ids_ref, g_ref, mine_ref, other_ref, *refs):
    *blocks, o_ref = refs

    def run(tokens_ref):
        tokens = tokens_ref[...]
        g = g_ref[...]
        total = jnp.zeros(o_ref.shape, jnp.float32)
        seen = 0
        for block in blocks:
            part = lax.dot_general(tokens, block[...], (((1,), (1,)), ((), ())), preferred_element_type=jnp.float32)
            for pair in range(block.shape[0] // (2 * rank)):
                ids = ids_of_pair(ids_ref, seen + 2 * pair, o_ref.shape, rank)
                total += jnp.where(g == ids, part[:, pair * 2 * rank : (pair + 1) * 2 * rank], 0.0)
            seen += block.shape[0] // rank
        o_ref[...] = total

    @pl.when(pl.program_id(0) < steps)
    def _():
        run(mine_ref)

    @pl.when(pl.program_id(0) >= steps)
    def _():
        run(other_ref)


def shrink(mine, other, g, ids, blocks):
    rows, width = mine.shape
    rank = blocks[0].shape[1]
    tile = min(256, rows)
    steps = rows // tile
    flat = [block.reshape(-1, width) for block in blocks]
    deep = sum(block.shape[0] for block in flat)
    return pl.pallas_call(
        functools.partial(shrink_kernel, rank, steps),
        out_shape=jax.ShapeDtypeStruct((2 * rows, 2 * rank), jnp.float32),
        grid_spec=pltpu.PrefetchScalarGridSpec(
            num_scalar_prefetch=1,
            grid=(2 * steps,),
            in_specs=[
                pl.BlockSpec((tile, 1), lambda i, ids: (i, 0)),
                pl.BlockSpec((tile, width), lambda i, ids: (jnp.minimum(i, steps - 1), 0)),
                pl.BlockSpec((tile, width), lambda i, ids: (jnp.maximum(i - steps, 0), 0)),
            ]
            + [pl.BlockSpec(block.shape, lambda i, ids: (0, 0)) for block in flat],
            out_specs=pl.BlockSpec((tile, 2 * rank), lambda i, ids: (i, 0)),
        ),
        compiler_params=pltpu.CompilerParams(vmem_limit_bytes=VMEM),
        cost_estimate=pl.CostEstimate(flops=1, bytes_accessed=1, transcendentals=0),
    )(ids, g, mine, other, *flat)


def expand_kernel(rank, ids_ref, g_ref, low_ref, base_ref, *refs):
    *blocks, o_ref, spread_ref = refs

    @pl.when(pl.program_id(0) == 0)
    def _():
        g = g_ref[...]
        low = low_ref[...].astype(jnp.float32)
        for pair in range(spread_ref.shape[1] // (2 * rank)):
            ids = ids_of_pair(ids_ref, 2 * pair, low.shape, rank)
            picked = jnp.where(g == ids, low, 0.0).astype(jnp.bfloat16)
            spread_ref[:, pair * 2 * rank : (pair + 1) * 2 * rank] = picked

    total = jnp.zeros(o_ref.shape, jnp.float32)
    seen = 0
    for block in blocks:
        deep = block.shape[0]
        total += jnp.dot(spread_ref[:, seen : seen + deep], block[...], preferred_element_type=jnp.float32)
        seen += deep
    o_ref[...] = base_ref[...] + adapter_scale * total


def expand(base, low, g, ids, blocks):
    rows = g.shape[0]
    _, rank, width = blocks[0].shape
    tile = min(512, width)
    flat = [block.reshape(-1, width) for block in blocks]
    deep = sum(block.shape[0] for block in flat)
    return pl.pallas_call(
        functools.partial(expand_kernel, rank),
        out_shape=jax.ShapeDtypeStruct((rows, width), jnp.float32),
        grid_spec=pltpu.PrefetchScalarGridSpec(
            num_scalar_prefetch=1,
            grid=(width // tile,),
            in_specs=[
                pl.BlockSpec((rows, 1), lambda i, ids: (0, 0)),
                pl.BlockSpec((rows, 2 * rank), lambda i, ids: (0, 0)),
                pl.BlockSpec((rows, tile), lambda i, ids: (0, i)),
            ]
            + [pl.BlockSpec((block.shape[0], tile), lambda i, ids: (0, i)) for block in flat],
            out_specs=pl.BlockSpec((rows, tile), lambda i, ids: (0, i)),
            scratch_shapes=[pltpu.VMEM((rows, deep), jnp.bfloat16)],
        ),
        compiler_params=pltpu.CompilerParams(vmem_limit_bytes=VMEM),
        cost_estimate=pl.CostEstimate(flops=1, bytes_accessed=1, transcendentals=0),
    )(ids, g, low, base, *flat)


def after(value, *others):
    return lax.optimization_barrier((value, *others))[0]


def wire(total):
    return total.astype(jnp.float16)


def unwire(block):
    return block.astype(jnp.float32)


def by_slots(line, z, weight, tokens):
    width = weight.shape[1] // line

    def sums(target):
        block = lax.dynamic_slice(weight, (0, target * width), (weight.shape[0], width))
        return BASE_WIRE * jnp.dot(tokens, block, preferred_element_type=jnp.float32)

    right = left = 0.0
    for slot in range(1, line):
        ahead, behind = (z - slot) % line, (z + slot) % line
        if 2 * slot <= line:
            one = sums(jnp.where(z < slot, ahead, behind))
            to_right, to_left = one + right, one + left
        else:
            to_right, to_left = sums(ahead) + right, sums(behind) + left
        going_right = [(i, i + 1) for i in range(slot)]
        going_left = [(line - 1 - i, line - 2 - i) for i in range(slot)]
        right = unwire(lax.ppermute(wire(to_right), "tensor", going_right))
        left = unwire(lax.ppermute(wire(to_left), "tensor", going_left))
    return right + left + sums(z)


def on_device(tokens, weight, down_stack, up_stack, fetch_list, choose):
    line = lax.axis_size("tensor")
    owners = lax.axis_size("dp")
    groups = lax.axis_size("groups")
    chips = owners // CORES
    z = lax.axis_index("tensor")
    me = lax.axis_index("dp")
    group = lax.axis_index("groups")
    x, core = me // CORES, me % CORES
    own, rank, width = down_stack.shape
    rows = tokens.shape[0]
    per_owner = fetch_list.shape[2]
    sibling = [(i, i ^ 1) for i in range(owners)]

    def to_sibling(block):
        return lax.ppermute(block, "dp", sibling)

    wanted = (jnp.arange(owners, dtype=jnp.int32)[:, None] * own + fetch_list[0]).reshape(-1)
    picked = choose[:, None] == jnp.arange(owners * per_owner, dtype=jnp.int32)[None, :]
    g = jnp.sum(jnp.where(picked, wanted[None, :], 0), axis=1)

    share = own // groups
    size = share // BANK_PIECES

    def slots(owner, first, count):
        return owner * own + first + jnp.arange(count, dtype=jnp.int32)

    def cross(stack, shift, piece, *gates):
        first = group * share + piece * size
        block = lax.dynamic_slice(stack, (first, 0, 0), (size, rank, width))
        block = lax.ppermute(after(block, *gates), "dp", [(i, (i + shift * CORES) % owners) for i in range(owners)])
        return block, slots((x - shift) % chips * CORES + core, first, size)

    def turn(block, shift, piece):
        found = []
        for step in range(1, groups):
            other = lax.ppermute(block, "groups", [(i, (i + step) % groups) for i in range(groups)])
            first = (group - step) % groups * share + piece * size
            found.append((other, slots((x - shift) % chips * CORES + core, first, size)))
        return found

    def shared(pairs):
        theirs = [(to_sibling(block), ids + jnp.where(core == 0, own, -own)) for block, ids in pairs]
        return pairs + theirs

    def product(target, rows_of):
        block = lax.dynamic_slice(weight, (0, target * width), (weight.shape[0], width))
        return BASE_WIRE * jnp.dot(rows_of, block, preferred_element_type=jnp.float32)

    mine = slots(me, 0, own)

    def shrink_by(tokens, tokens_other, g_both, pairs):
        ids = jnp.concatenate([ids for _, ids in pairs])
        return shrink(tokens, tokens_other, g_both, ids, [block for block, _ in pairs])

    def joined(halves):
        part = halves[:, :rank] + halves[:, rank:]
        part = part[:rows] + to_sibling(part[rows:])
        return jnp.concatenate([part[: rows // 2], part[rows // 2 :]], axis=1)

    def update(base, low, pairs):
        low = jnp.concatenate([low[:, :rank], low[:, rank:]], axis=0)
        ids = jnp.concatenate([ids for _, ids in pairs])
        return expand(base, jnp.concatenate([low, low], axis=1), g[:, None], ids, [block for block, _ in pairs])

    if line != 4 or chips != 2 or groups != 2:
        summed = by_slots(line, z, weight, tokens) * (1.0 / BASE_WIRE)
        g_both = jnp.concatenate([g, to_sibling(g)])[:, None]
        banks = []
        for stack in (down_stack, up_stack):
            pairs = [(stack, mine)]
            for shift in range(1, chips):
                for piece in range(BANK_PIECES):
                    block, ids = cross(stack, shift, piece)
                    pairs += [(block, ids), *turn(block, shift, piece)]
            banks.append(pairs)
        part = joined(shrink_by(tokens, to_sibling(tokens), g_both, banks[0]))
        low = lax.psum(part, "tensor").astype(jnp.bfloat16)
        return update(summed, low, shared(banks[1])).astype(jnp.bfloat16)

    outer = [(0, 1), (3, 2)]
    inner = [(1, 2), (2, 1)]
    both = [(0, 1), (1, 0), (2, 3), (3, 2)]
    low_half = z < 2
    targets = [jnp.where(low_half, 3, 0), jnp.where(low_half, 2, 1), jnp.array([1, 0, 3, 2], jnp.int32)[z]]

    def hop(block, pairs):
        return lax.ppermute(block, "tensor", pairs)

    def part_of(block, span):
        return lax.slice_in_dim(block, span[0], span[0] + span[1])

    spans = [(0, rows * 3 // 8), (rows * 3 // 8, rows * 5 // 8)]
    d0, d0_ids = cross(down_stack, 1, 0)
    up_other = to_sibling(up_stack)
    first = wire(product(targets[0], tokens))
    first, tokens, g, down, up, up_other = lax.optimization_barrier(
        (first, tokens, g, down_stack, up_stack, up_other)
    )

    a1 = hop(first, outer)
    g_other, tokens_other = to_sibling(g), to_sibling(tokens)
    later = after(tokens, g_other, tokens_other)
    second = wire(product(targets[1], later))
    d0 = after(d0, second)
    d1, d1_ids = cross(down, 1, 1, d0)
    [(d2, d2_ids)] = turn(d0, 1, 0)
    third = wire(product(targets[2], after(later, d0)))
    g_both = jnp.concatenate([g, g_other])[:, None]
    first, second, third, a1, tokens, tokens_other = lax.optimization_barrier(
        (first, second, third, a1, tokens, tokens_other)
    )

    d1 = after(d1, a1)

    a2 = hop(second, outer)
    b1 = hop(wire(unwire(first) + unwire(a1)), inner)
    [(d3, d3_ids)] = turn(d1, 1, 1)
    u0, u0_ids = cross(up, 1, 0, d1)
    u1, u1_ids = cross(up, 1, 1, u0)
    halves = shrink_by(after(tokens, d2), tokens_other, g_both, [(down_stack, mine)])
    home = product(z, tokens) * (1.0 / BASE_WIRE)
    later = after(tokens, home)
    halves += shrink_by(later, tokens_other, g_both, [(d0, d0_ids), (d1, d1_ids), (d2, d2_ids), (d3, d3_ids)])
    part = joined(halves)
    [(u2, u2_ids)] = turn(u0, 1, 0)
    ups = [(up, mine), (up_other, slots(me ^ 1, 0, own)), *shared([(u0, u0_ids), (u1, u1_ids), (u2, u2_ids)])]
    late = turn(u1, 1, 1)
    part += hop(after(part, a2), both)
    c1 = [wire(unwire(part_of(third, span)) + unwire(part_of(b1, span))) for span in spans]
    b2 = wire(unwire(second) + unwire(a2))
    part, c1[0], home, *seen = lax.optimization_barrier((part, c1[0], home, *[block for block, _ in ups]))
    ups = [(block, ids) for block, (_, ids) in zip(seen, ups)]

    a3 = [hop(block, both) for block in c1]
    part += hop(part, inner)
    b2 = hop(after(b2, part), inner)
    low = part.astype(jnp.bfloat16)
    low = jnp.where((z == 1) | (z == 2), low, hop(low, [(1, 0), (2, 3)]))
    adapted = update(home, after(low, a3[0]), ups)
    adapted = update(adapted, low, shared(late))
    out = jnp.zeros((rows, width), jnp.bfloat16)
    for arrived, span in zip(a3, spans):
        wired = unwire(arrived) + unwire(part_of(b2, span))
        total = part_of(adapted, span) + wired * (1.0 / BASE_WIRE)
        out = lax.dynamic_update_slice(lax.optimization_barrier(out), total.astype(jnp.bfloat16), (span[0], 0))
    return out


def solution(mesh):
    return jax.shard_map(
        on_device,
        mesh=mesh,
        in_specs=(
            P(("groups", "dp"), "tensor"),
            P("tensor", None),
            P("dp", None, "tensor"),
            P("dp", None, "tensor"),
            P(("groups", "dp"), None, None),
            P(("groups", "dp")),
        ),
        out_specs=P(("groups", "dp"), "tensor"),
        check_vma=False,
    )
```

```python
import functools

import jax
import jax.numpy as jnp
from jax import lax
from jax.experimental import pallas as pl
from jax.experimental.pallas import tpu as pltpu
from jax.sharding import PartitionSpec as P

adapter_scale = 0.5
CORES = 2
BANK_PIECES = 2
BASE_WIRE = 8.0
VMEM = 48 * 1024 * 1024


def ids_of_pair(ids_ref, first, shape, rank):
    lane = lax.broadcasted_iota(jnp.int32, shape, 1)
    return jnp.where(lane < rank, ids_ref[first], ids_ref[first + 1])


def shrink_kernel(rank, steps, ids_ref, g_ref, mine_ref, other_ref, *refs):
    *blocks, o_ref = refs

    def run(tokens_ref):
        tokens = tokens_ref[...]
        g = g_ref[...]
        total = jnp.zeros(o_ref.shape, jnp.float32)
        seen = 0
        for block in blocks:
            part = lax.dot_general(tokens, block[...], (((1,), (1,)), ((), ())), preferred_element_type=jnp.float32)
            for pair in range(block.shape[0] // (2 * rank)):
                ids = ids_of_pair(ids_ref, seen + 2 * pair, o_ref.shape, rank)
                total += jnp.where(g == ids, part[:, pair * 2 * rank : (pair + 1) * 2 * rank], 0.0)
            seen += block.shape[0] // rank
        o_ref[...] = total

    @pl.when(pl.program_id(0) < steps)
    def _():
        run(mine_ref)

    @pl.when(pl.program_id(0) >= steps)
    def _():
        run(other_ref)


def shrink(mine, other, g, ids, blocks):
    rows, width = mine.shape
    rank = blocks[0].shape[1]
    tile = min(256, rows)
    steps = rows // tile
    flat = [block.reshape(-1, width) for block in blocks]
    deep = sum(block.shape[0] for block in flat)
    return pl.pallas_call(
        functools.partial(shrink_kernel, rank, steps),
        out_shape=jax.ShapeDtypeStruct((2 * rows, 2 * rank), jnp.float32),
        grid_spec=pltpu.PrefetchScalarGridSpec(
            num_scalar_prefetch=1,
            grid=(2 * steps,),
            in_specs=[
                pl.BlockSpec((tile, 1), lambda i, ids: (i, 0)),
                pl.BlockSpec((tile, width), lambda i, ids: (jnp.minimum(i, steps - 1), 0)),
                pl.BlockSpec((tile, width), lambda i, ids: (jnp.maximum(i - steps, 0), 0)),
            ]
            + [pl.BlockSpec(block.shape, lambda i, ids: (0, 0)) for block in flat],
            out_specs=pl.BlockSpec((tile, 2 * rank), lambda i, ids: (i, 0)),
        ),
        compiler_params=pltpu.CompilerParams(vmem_limit_bytes=VMEM),
        cost_estimate=pl.CostEstimate(flops=1, bytes_accessed=1, transcendentals=0),
    )(ids, g, mine, other, *flat)


def expand_kernel(rank, ids_ref, g_ref, low_ref, base_ref, *refs):
    *blocks, o_ref, spread_ref = refs

    @pl.when(pl.program_id(0) == 0)
    def _():
        g = g_ref[...]
        low = low_ref[...].astype(jnp.float32)
        for pair in range(spread_ref.shape[1] // (2 * rank)):
            ids = ids_of_pair(ids_ref, 2 * pair, low.shape, rank)
            picked = jnp.where(g == ids, low, 0.0).astype(jnp.bfloat16)
            spread_ref[:, pair * 2 * rank : (pair + 1) * 2 * rank] = picked

    total = jnp.zeros(o_ref.shape, jnp.float32)
    seen = 0
    for block in blocks:
        deep = block.shape[0]
        total += jnp.dot(spread_ref[:, seen : seen + deep], block[...], preferred_element_type=jnp.float32)
        seen += deep
    o_ref[...] = base_ref[...] + adapter_scale * total


def expand(base, low, g, ids, blocks):
    rows = g.shape[0]
    _, rank, width = blocks[0].shape
    tile = min(512, width)
    flat = [block.reshape(-1, width) for block in blocks]
    deep = sum(block.shape[0] for block in flat)
    return pl.pallas_call(
        functools.partial(expand_kernel, rank),
        out_shape=jax.ShapeDtypeStruct((rows, width), jnp.float32),
        grid_spec=pltpu.PrefetchScalarGridSpec(
            num_scalar_prefetch=1,
            grid=(width // tile,),
            in_specs=[
                pl.BlockSpec((rows, 1), lambda i, ids: (0, 0)),
                pl.BlockSpec((rows, 2 * rank), lambda i, ids: (0, 0)),
                pl.BlockSpec((rows, tile), lambda i, ids: (0, i)),
            ]
            + [pl.BlockSpec((block.shape[0], tile), lambda i, ids: (0, i)) for block in flat],
            out_specs=pl.BlockSpec((rows, tile), lambda i, ids: (0, i)),
            scratch_shapes=[pltpu.VMEM((rows, deep), jnp.bfloat16)],
        ),
        compiler_params=pltpu.CompilerParams(vmem_limit_bytes=VMEM),
        cost_estimate=pl.CostEstimate(flops=1, bytes_accessed=1, transcendentals=0),
    )(ids, g, low, base, *flat)


def after(value, *others):
    return lax.optimization_barrier((value, *others))[0]


def wire(total):
    return total.astype(jnp.float16)


def unwire(block):
    return block.astype(jnp.float32)


def by_slots(line, z, weight, tokens):
    width = weight.shape[1] // line

    def sums(target):
        block = lax.dynamic_slice(weight, (0, target * width), (weight.shape[0], width))
        return BASE_WIRE * jnp.dot(tokens, block, preferred_element_type=jnp.float32)

    right = left = 0.0
    for slot in range(1, line):
        ahead, behind = (z - slot) % line, (z + slot) % line
        if 2 * slot <= line:
            one = sums(jnp.where(z < slot, ahead, behind))
            to_right, to_left = one + right, one + left
        else:
            to_right, to_left = sums(ahead) + right, sums(behind) + left
        going_right = [(i, i + 1) for i in range(slot)]
        going_left = [(line - 1 - i, line - 2 - i) for i in range(slot)]
        right = unwire(lax.ppermute(wire(to_right), "tensor", going_right))
        left = unwire(lax.ppermute(wire(to_left), "tensor", going_left))
    return right + left + sums(z)


def on_device(tokens, weight, down_stack, up_stack, fetch_list, choose):
    line = lax.axis_size("tensor")
    owners = lax.axis_size("dp")
    groups = lax.axis_size("groups")
    chips = owners // CORES
    z = lax.axis_index("tensor")
    me = lax.axis_index("dp")
    group = lax.axis_index("groups")
    x, core = me // CORES, me % CORES
    own, rank, width = down_stack.shape
    rows = tokens.shape[0]
    per_owner = fetch_list.shape[2]
    sibling = [(i, i ^ 1) for i in range(owners)]

    def to_sibling(block):
        return lax.ppermute(block, "dp", sibling)

    wanted = (jnp.arange(owners, dtype=jnp.int32)[:, None] * own + fetch_list[0]).reshape(-1)
    picked = choose[:, None] == jnp.arange(owners * per_owner, dtype=jnp.int32)[None, :]
    g = jnp.sum(jnp.where(picked, wanted[None, :], 0), axis=1)

    share = own // groups
    size = share // BANK_PIECES

    def slots(owner, first, count):
        return owner * own + first + jnp.arange(count, dtype=jnp.int32)

    def cross(stack, shift, piece, *gates):
        first = group * share + piece * size
        block = lax.dynamic_slice(stack, (first, 0, 0), (size, rank, width))
        block = lax.ppermute(after(block, *gates), "dp", [(i, (i + shift * CORES) % owners) for i in range(owners)])
        return block, slots((x - shift) % chips * CORES + core, first, size)

    def turn(block, shift, piece):
        found = []
        for step in range(1, groups):
            other = lax.ppermute(block, "groups", [(i, (i + step) % groups) for i in range(groups)])
            first = (group - step) % groups * share + piece * size
            found.append((other, slots((x - shift) % chips * CORES + core, first, size)))
        return found

    def shared(pairs):
        theirs = [(to_sibling(block), ids + jnp.where(core == 0, own, -own)) for block, ids in pairs]
        return pairs + theirs

    def product(target, rows_of):
        block = lax.dynamic_slice(weight, (0, target * width), (weight.shape[0], width))
        return BASE_WIRE * jnp.dot(rows_of, block, preferred_element_type=jnp.float32)

    mine = slots(me, 0, own)

    def shrink_by(tokens, tokens_other, g_both, pairs):
        ids = jnp.concatenate([ids for _, ids in pairs])
        return shrink(tokens, tokens_other, g_both, ids, [block for block, _ in pairs])

    def joined(halves):
        part = halves[:, :rank] + halves[:, rank:]
        part = part[:rows] + to_sibling(part[rows:])
        return jnp.concatenate([part[: rows // 2], part[rows // 2 :]], axis=1)

    def update(base, low, pairs):
        low = jnp.concatenate([low[:, :rank], low[:, rank:]], axis=0)
        ids = jnp.concatenate([ids for _, ids in pairs])
        return expand(base, jnp.concatenate([low, low], axis=1), g[:, None], ids, [block for block, _ in pairs])

    if line != 4 or chips != 2 or groups != 2:
        summed = by_slots(line, z, weight, tokens) * (1.0 / BASE_WIRE)
        g_both = jnp.concatenate([g, to_sibling(g)])[:, None]
        banks = []
        for stack in (down_stack, up_stack):
            pairs = [(stack, mine)]
            for shift in range(1, chips):
                for piece in range(BANK_PIECES):
                    block, ids = cross(stack, shift, piece)
                    pairs += [(block, ids), *turn(block, shift, piece)]
            banks.append(pairs)
        part = joined(shrink_by(tokens, to_sibling(tokens), g_both, banks[0]))
        low = lax.psum(part, "tensor").astype(jnp.bfloat16)
        return update(summed, low, shared(banks[1])).astype(jnp.bfloat16)

    outer = [(0, 1), (3, 2)]
    inner = [(1, 2), (2, 1)]
    both = [(0, 1), (1, 0), (2, 3), (3, 2)]
    low_half = z < 2
    targets = [jnp.where(low_half, 3, 0), jnp.where(low_half, 2, 1), jnp.array([1, 0, 3, 2], jnp.int32)[z]]

    def hop(block, pairs):
        return lax.ppermute(block, "tensor", pairs)

    def part_of(block, span):
        return lax.slice_in_dim(block, span[0], span[0] + span[1])

    spans = [(0, rows // 4), (rows // 4, rows * 3 // 4)]
    d0, d0_ids = cross(down_stack, 1, 0)
    up_other = to_sibling(up_stack)
    first = wire(product(targets[0], tokens))
    first, tokens, g, down, up, up_other = lax.optimization_barrier(
        (first, tokens, g, down_stack, up_stack, up_other)
    )

    a1 = hop(first, outer)
    g_other, tokens_other = to_sibling(g), to_sibling(tokens)
    later = after(tokens, g_other, tokens_other)
    second = wire(product(targets[1], later))
    d0 = after(d0, second)
    d1, d1_ids = cross(down, 1, 1, d0)
    [(d2, d2_ids)] = turn(d0, 1, 0)
    third = wire(product(targets[2], after(later, d0)))
    g_both = jnp.concatenate([g, g_other])[:, None]
    first, second, third, a1, tokens, tokens_other, d1, d2 = lax.optimization_barrier(
        (first, second, third, a1, tokens, tokens_other, d1, d2)
    )

    a2 = hop(second, outer)
    b1 = hop(wire(unwire(first) + unwire(a1)), inner)
    [(d3, d3_ids)] = turn(d1, 1, 1)
    u0, u0_ids = cross(up, 1, 0, d1)
    halves = shrink_by(tokens, tokens_other, g_both, [(down_stack, mine)])
    u0 = after(u0, halves)
    u1, u1_ids = cross(up, 1, 1, u0)
    home = product(z, tokens) * (1.0 / BASE_WIRE)
    later = after(tokens, home)
    halves += shrink_by(later, tokens_other, g_both, [(d0, d0_ids), (d1, d1_ids), (d2, d2_ids), (d3, d3_ids)])
    part = joined(halves)
    [(u2, u2_ids)] = turn(u0, 1, 0)
    ups = [(up, mine), (up_other, slots(me ^ 1, 0, own)), *shared([(u0, u0_ids)])]
    part += hop(after(part, a2), both)
    c1 = [wire(unwire(part_of(third, span)) + unwire(part_of(b1, span))) for span in spans]
    b2 = wire(unwire(second) + unwire(a2))
    part, c1[0], b2, home, u2, *seen = lax.optimization_barrier(
        (part, c1[0], b2, home, u2, *[block for block, _ in ups])
    )
    ups = [(block, ids) for block, (_, ids) in zip(seen, ups)]

    a3 = [hop(block, both) for block in c1]
    part += hop(part, inner)
    b2 = hop(after(b2, part), inner)
    u1 = after(u1, part)
    late = turn(u1, 1, 1)
    low = part.astype(jnp.bfloat16)
    low = jnp.where((z == 1) | (z == 2), low, hop(low, [(1, 0), (2, 3)]))
    u1, u2, low = lax.optimization_barrier((u1, u2, low, a3[0]))[:3]
    ups += shared([(u1, u1_ids), (u2, u2_ids)])
    adapted = update(home, low, ups)
    adapted = update(adapted, low, shared(late))
    out = jnp.zeros((rows, width), jnp.bfloat16)
    for arrived, span in zip(a3, spans):
        wired = unwire(arrived) + unwire(part_of(b2, span))
        total = part_of(adapted, span) + wired * (1.0 / BASE_WIRE)
        out = lax.dynamic_update_slice(lax.optimization_barrier(out), total.astype(jnp.bfloat16), (span[0], 0))
    return out


def solution(mesh):
    return jax.shard_map(
        on_device,
        mesh=mesh,
        in_specs=(
            P(("groups", "dp"), "tensor"),
            P("tensor", None),
            P("dp", None, "tensor"),
            P("dp", None, "tensor"),
            P(("groups", "dp"), None, None),
            P(("groups", "dp")),
        ),
        out_specs=P(("groups", "dp"), "tensor"),
        check_vma=False,
    )
```

```python
import functools

import jax
import jax.numpy as jnp
from jax import lax
from jax.experimental import pallas as pl
from jax.experimental.pallas import tpu as pltpu
from jax.sharding import PartitionSpec as P

adapter_scale = 0.5
CORES = 2
BANK_PIECES = 2
BASE_WIRE = 8.0
VMEM = 48 * 1024 * 1024


def ids_of_pair(ids_ref, first, shape, rank):
    lane = lax.broadcasted_iota(jnp.int32, shape, 1)
    return jnp.where(lane < rank, ids_ref[first], ids_ref[first + 1])


def shrink_kernel(rank, steps, ids_ref, g_ref, mine_ref, other_ref, *refs):
    *blocks, o_ref = refs

    def run(tokens_ref):
        tokens = tokens_ref[...]
        g = g_ref[...]
        total = jnp.zeros(o_ref.shape, jnp.float32)
        seen = 0
        for block in blocks:
            part = lax.dot_general(tokens, block[...], (((1,), (1,)), ((), ())), preferred_element_type=jnp.float32)
            for pair in range(block.shape[0] // (2 * rank)):
                ids = ids_of_pair(ids_ref, seen + 2 * pair, o_ref.shape, rank)
                total += jnp.where(g == ids, part[:, pair * 2 * rank : (pair + 1) * 2 * rank], 0.0)
            seen += block.shape[0] // rank
        o_ref[...] = total

    @pl.when(pl.program_id(0) < steps)
    def _():
        run(mine_ref)

    @pl.when(pl.program_id(0) >= steps)
    def _():
        run(other_ref)


def shrink(mine, other, g, ids, blocks):
    rows, width = mine.shape
    rank = blocks[0].shape[1]
    tile = min(256, rows)
    steps = rows // tile
    flat = [block.reshape(-1, width) for block in blocks]
    deep = sum(block.shape[0] for block in flat)
    return pl.pallas_call(
        functools.partial(shrink_kernel, rank, steps),
        out_shape=jax.ShapeDtypeStruct((2 * rows, 2 * rank), jnp.float32),
        grid_spec=pltpu.PrefetchScalarGridSpec(
            num_scalar_prefetch=1,
            grid=(2 * steps,),
            in_specs=[
                pl.BlockSpec((tile, 1), lambda i, ids: (i, 0)),
                pl.BlockSpec((tile, width), lambda i, ids: (jnp.minimum(i, steps - 1), 0)),
                pl.BlockSpec((tile, width), lambda i, ids: (jnp.maximum(i - steps, 0), 0)),
            ]
            + [pl.BlockSpec(block.shape, lambda i, ids: (0, 0)) for block in flat],
            out_specs=pl.BlockSpec((tile, 2 * rank), lambda i, ids: (i, 0)),
        ),
        compiler_params=pltpu.CompilerParams(vmem_limit_bytes=VMEM),
        cost_estimate=pl.CostEstimate(flops=1, bytes_accessed=1, transcendentals=0),
    )(ids, g, mine, other, *flat)


def expand_kernel(rank, ids_ref, g_ref, low_ref, base_ref, *refs):
    *blocks, o_ref, spread_ref = refs

    @pl.when(pl.program_id(0) == 0)
    def _():
        g = g_ref[...]
        low = low_ref[...].astype(jnp.float32)
        for pair in range(spread_ref.shape[1] // (2 * rank)):
            ids = ids_of_pair(ids_ref, 2 * pair, low.shape, rank)
            picked = jnp.where(g == ids, low, 0.0).astype(jnp.bfloat16)
            spread_ref[:, pair * 2 * rank : (pair + 1) * 2 * rank] = picked

    total = jnp.zeros(o_ref.shape, jnp.float32)
    seen = 0
    for block in blocks:
        deep = block.shape[0]
        total += jnp.dot(spread_ref[:, seen : seen + deep], block[...], preferred_element_type=jnp.float32)
        seen += deep
    o_ref[...] = base_ref[...] + adapter_scale * total


def expand(base, low, g, ids, blocks):
    rows = g.shape[0]
    _, rank, width = blocks[0].shape
    tile = min(512, width)
    flat = [block.reshape(-1, width) for block in blocks]
    deep = sum(block.shape[0] for block in flat)
    return pl.pallas_call(
        functools.partial(expand_kernel, rank),
        out_shape=jax.ShapeDtypeStruct((rows, width), jnp.float32),
        grid_spec=pltpu.PrefetchScalarGridSpec(
            num_scalar_prefetch=1,
            grid=(width // tile,),
            in_specs=[
                pl.BlockSpec((rows, 1), lambda i, ids: (0, 0)),
                pl.BlockSpec((rows, 2 * rank), lambda i, ids: (0, 0)),
                pl.BlockSpec((rows, tile), lambda i, ids: (0, i)),
            ]
            + [pl.BlockSpec((block.shape[0], tile), lambda i, ids: (0, i)) for block in flat],
            out_specs=pl.BlockSpec((rows, tile), lambda i, ids: (0, i)),
            scratch_shapes=[pltpu.VMEM((rows, deep), jnp.bfloat16)],
        ),
        compiler_params=pltpu.CompilerParams(vmem_limit_bytes=VMEM),
        cost_estimate=pl.CostEstimate(flops=1, bytes_accessed=1, transcendentals=0),
    )(ids, g, low, base, *flat)


def after(value, *others):
    return lax.optimization_barrier((value, *others))[0]


def wire(total):
    return total.astype(jnp.float16)


def unwire(block):
    return block.astype(jnp.float32)


def by_slots(line, z, weight, tokens):
    width = weight.shape[1] // line

    def sums(target):
        block = lax.dynamic_slice(weight, (0, target * width), (weight.shape[0], width))
        return BASE_WIRE * jnp.dot(tokens, block, preferred_element_type=jnp.float32)

    right = left = 0.0
    for slot in range(1, line):
        ahead, behind = (z - slot) % line, (z + slot) % line
        if 2 * slot <= line:
            one = sums(jnp.where(z < slot, ahead, behind))
            to_right, to_left = one + right, one + left
        else:
            to_right, to_left = sums(ahead) + right, sums(behind) + left
        going_right = [(i, i + 1) for i in range(slot)]
        going_left = [(line - 1 - i, line - 2 - i) for i in range(slot)]
        right = unwire(lax.ppermute(wire(to_right), "tensor", going_right))
        left = unwire(lax.ppermute(wire(to_left), "tensor", going_left))
    return right + left + sums(z)


def on_device(tokens, weight, down_stack, up_stack, fetch_list, choose):
    line = lax.axis_size("tensor")
    owners = lax.axis_size("dp")
    groups = lax.axis_size("groups")
    chips = owners // CORES
    z = lax.axis_index("tensor")
    me = lax.axis_index("dp")
    group = lax.axis_index("groups")
    x, core = me // CORES, me % CORES
    own, rank, width = down_stack.shape
    rows = tokens.shape[0]
    per_owner = fetch_list.shape[2]
    sibling = [(i, i ^ 1) for i in range(owners)]

    def to_sibling(block):
        return lax.ppermute(block, "dp", sibling)

    wanted = (jnp.arange(owners, dtype=jnp.int32)[:, None] * own + fetch_list[0]).reshape(-1)
    picked = choose[:, None] == jnp.arange(owners * per_owner, dtype=jnp.int32)[None, :]
    g = jnp.sum(jnp.where(picked, wanted[None, :], 0), axis=1)

    share = own // groups
    size = share // BANK_PIECES

    def slots(owner, first, count):
        return owner * own + first + jnp.arange(count, dtype=jnp.int32)

    def cross(stack, shift, piece, *gates):
        first = group * share + piece * size
        block = lax.dynamic_slice(stack, (first, 0, 0), (size, rank, width))
        block = lax.ppermute(after(block, *gates), "dp", [(i, (i + shift * CORES) % owners) for i in range(owners)])
        return block, slots((x - shift) % chips * CORES + core, first, size)

    def turn(block, shift, piece):
        found = []
        for step in range(1, groups):
            other = lax.ppermute(block, "groups", [(i, (i + step) % groups) for i in range(groups)])
            first = (group - step) % groups * share + piece * size
            found.append((other, slots((x - shift) % chips * CORES + core, first, size)))
        return found

    def shared(pairs):
        theirs = [(to_sibling(block), ids + jnp.where(core == 0, own, -own)) for block, ids in pairs]
        return pairs + theirs

    def product(target, rows_of):
        block = lax.dynamic_slice(weight, (0, target * width), (weight.shape[0], width))
        return BASE_WIRE * jnp.dot(rows_of, block, preferred_element_type=jnp.float32)

    mine = slots(me, 0, own)

    def shrink_by(tokens, tokens_other, g_both, pairs):
        ids = jnp.concatenate([ids for _, ids in pairs])
        return shrink(tokens, tokens_other, g_both, ids, [block for block, _ in pairs])

    def joined(halves):
        part = halves[:, :rank] + halves[:, rank:]
        part = part[:rows] + to_sibling(part[rows:])
        return jnp.concatenate([part[: rows // 2], part[rows // 2 :]], axis=1)

    def update(base, low, pairs):
        low = jnp.concatenate([low[:, :rank], low[:, rank:]], axis=0)
        ids = jnp.concatenate([ids for _, ids in pairs])
        return expand(base, jnp.concatenate([low, low], axis=1), g[:, None], ids, [block for block, _ in pairs])

    if line != 4 or chips != 2 or groups != 2:
        summed = by_slots(line, z, weight, tokens) * (1.0 / BASE_WIRE)
        g_both = jnp.concatenate([g, to_sibling(g)])[:, None]
        banks = []
        for stack in (down_stack, up_stack):
            pairs = [(stack, mine)]
            for shift in range(1, chips):
                for piece in range(BANK_PIECES):
                    block, ids = cross(stack, shift, piece)
                    pairs += [(block, ids), *turn(block, shift, piece)]
            banks.append(pairs)
        part = joined(shrink_by(tokens, to_sibling(tokens), g_both, banks[0]))
        low = lax.psum(part, "tensor").astype(jnp.bfloat16)
        return update(summed, low, shared(banks[1])).astype(jnp.bfloat16)

    outer = [(0, 1), (3, 2)]
    inner = [(1, 2), (2, 1)]
    both = [(0, 1), (1, 0), (2, 3), (3, 2)]
    low_half = z < 2
    targets = [jnp.where(low_half, 3, 0), jnp.where(low_half, 2, 1), jnp.array([1, 0, 3, 2], jnp.int32)[z]]

    def hop(block, pairs):
        return lax.ppermute(block, "tensor", pairs)

    def part_of(block, span):
        return lax.slice_in_dim(block, span[0], span[0] + span[1])

    spans = [(0, rows // 4), (rows // 4, rows * 3 // 4)]
    d0, d0_ids = cross(down_stack, 1, 0)
    up_other = to_sibling(up_stack)
    first = wire(product(targets[0], tokens))
    first, tokens, g, down, up, up_other = lax.optimization_barrier(
        (first, tokens, g, down_stack, up_stack, up_other)
    )

    a1 = hop(first, outer)
    g_other, tokens_other = to_sibling(g), to_sibling(tokens)
    later = after(tokens, g_other, tokens_other)
    second = wire(product(targets[1], later))
    d0 = after(d0, second)
    d1, d1_ids = cross(down, 1, 1, d0)
    [(d2, d2_ids)] = turn(d0, 1, 0)
    third = wire(product(targets[2], after(later, d0)))
    g_both = jnp.concatenate([g, g_other])[:, None]
    first, second, third, a1, tokens, tokens_other, d1, d2 = lax.optimization_barrier(
        (first, second, third, a1, tokens, tokens_other, d1, d2)
    )

    a2 = hop(second, outer)
    b1 = hop(wire(unwire(first) + unwire(a1)), inner)
    [(d3, d3_ids)] = turn(d1, 1, 1)
    u0, u0_ids = cross(up, 1, 0, d1)
    halves = shrink_by(tokens, tokens_other, g_both, [(down_stack, mine)])
    u0 = after(u0, halves)
    u1, u1_ids = cross(up, 1, 1, u0)
    home = product(z, tokens) * (1.0 / BASE_WIRE)
    later = after(tokens, home)
    halves += shrink_by(later, tokens_other, g_both, [(d0, d0_ids), (d1, d1_ids), (d2, d2_ids), (d3, d3_ids)])
    part = joined(halves)
    [(u2, u2_ids)] = turn(u0, 1, 0)
    ups = [(up, mine), (up_other, slots(me ^ 1, 0, own)), *shared([(u0, u0_ids)])]
    part += hop(after(part, a2), both)
    c1 = [wire(unwire(part_of(third, span)) + unwire(part_of(b1, span))) for span in spans]
    b2 = wire(unwire(second) + unwire(a2))
    part, c1[0], b2, home, *seen = lax.optimization_barrier((part, c1[0], b2, home, *[block for block, _ in ups]))
    ups = [(block, ids) for block, (_, ids) in zip(seen, ups)]

    a3 = [hop(after(block, u2), both) for block in c1]
    part += hop(part, inner)
    b2 = hop(after(b2, part, u2), inner)
    u1 = after(u1, part)
    late = turn(u1, 1, 1)
    low = part.astype(jnp.bfloat16)
    low = jnp.where((z == 1) | (z == 2), low, hop(low, [(1, 0), (2, 3)]))
    u1, u2, low = lax.optimization_barrier((u1, u2, low, a3[0]))[:3]
    ups += shared([(u1, u1_ids), (u2, u2_ids)])
    adapted = update(home, low, ups)
    adapted = update(adapted, low, shared(late))
    out = jnp.zeros((rows, width), jnp.bfloat16)
    for arrived, span in zip(a3, spans):
        wired = unwire(arrived) + unwire(part_of(b2, span))
        total = part_of(adapted, span) + wired * (1.0 / BASE_WIRE)
        out = lax.dynamic_update_slice(lax.optimization_barrier(out), total.astype(jnp.bfloat16), (span[0], 0))
    return out


def solution(mesh):
    return jax.shard_map(
        on_device,
        mesh=mesh,
        in_specs=(
            P(("groups", "dp"), "tensor"),
            P("tensor", None),
            P("dp", None, "tensor"),
            P("dp", None, "tensor"),
            P(("groups", "dp"), None, None),
            P(("groups", "dp")),
        ),
        out_specs=P(("groups", "dp"), "tensor"),
        check_vma=False,
    )
```

```python
import functools

import jax
import jax.numpy as jnp
from jax import lax
from jax.experimental import pallas as pl
from jax.experimental.pallas import tpu as pltpu
from jax.sharding import PartitionSpec as P

adapter_scale = 0.5
CORES = 2
BANK_PIECES = 2
BASE_WIRE = 8.0
VMEM = 48 * 1024 * 1024


def ids_of_pair(ids_ref, first, shape, rank):
    lane = lax.broadcasted_iota(jnp.int32, shape, 1)
    return jnp.where(lane < rank, ids_ref[first], ids_ref[first + 1])


def shrink_kernel(rank, steps, ids_ref, g_ref, mine_ref, other_ref, *refs):
    *blocks, o_ref = refs

    def run(tokens_ref):
        tokens = tokens_ref[...]
        g = g_ref[...]
        total = jnp.zeros(o_ref.shape, jnp.float32)
        seen = 0
        for block in blocks:
            part = lax.dot_general(tokens, block[...], (((1,), (1,)), ((), ())), preferred_element_type=jnp.float32)
            for pair in range(block.shape[0] // (2 * rank)):
                ids = ids_of_pair(ids_ref, seen + 2 * pair, o_ref.shape, rank)
                total += jnp.where(g == ids, part[:, pair * 2 * rank : (pair + 1) * 2 * rank], 0.0)
            seen += block.shape[0] // rank
        o_ref[...] = total

    @pl.when(pl.program_id(0) < steps)
    def _():
        run(mine_ref)

    @pl.when(pl.program_id(0) >= steps)
    def _():
        run(other_ref)


def shrink(mine, other, g, ids, blocks):
    rows, width = mine.shape
    rank = blocks[0].shape[1]
    tile = min(256, rows)
    steps = rows // tile
    flat = [block.reshape(-1, width) for block in blocks]
    deep = sum(block.shape[0] for block in flat)
    return pl.pallas_call(
        functools.partial(shrink_kernel, rank, steps),
        out_shape=jax.ShapeDtypeStruct((2 * rows, 2 * rank), jnp.float32),
        grid_spec=pltpu.PrefetchScalarGridSpec(
            num_scalar_prefetch=1,
            grid=(2 * steps,),
            in_specs=[
                pl.BlockSpec((tile, 1), lambda i, ids: (i, 0)),
                pl.BlockSpec((tile, width), lambda i, ids: (jnp.minimum(i, steps - 1), 0)),
                pl.BlockSpec((tile, width), lambda i, ids: (jnp.maximum(i - steps, 0), 0)),
            ]
            + [pl.BlockSpec(block.shape, lambda i, ids: (0, 0)) for block in flat],
            out_specs=pl.BlockSpec((tile, 2 * rank), lambda i, ids: (i, 0)),
        ),
        compiler_params=pltpu.CompilerParams(vmem_limit_bytes=VMEM),
        cost_estimate=pl.CostEstimate(flops=1, bytes_accessed=1, transcendentals=0),
    )(ids, g, mine, other, *flat)


def expand_kernel(rank, ids_ref, g_ref, low_ref, base_ref, *refs):
    *blocks, o_ref, spread_ref = refs

    @pl.when(pl.program_id(0) == 0)
    def _():
        g = g_ref[...]
        low = low_ref[...].astype(jnp.float32)
        for pair in range(spread_ref.shape[1] // (2 * rank)):
            ids = ids_of_pair(ids_ref, 2 * pair, low.shape, rank)
            picked = jnp.where(g == ids, low, 0.0).astype(jnp.bfloat16)
            spread_ref[:, pair * 2 * rank : (pair + 1) * 2 * rank] = picked

    total = jnp.zeros(o_ref.shape, jnp.float32)
    seen = 0
    for block in blocks:
        deep = block.shape[0]
        total += jnp.dot(spread_ref[:, seen : seen + deep], block[...], preferred_element_type=jnp.float32)
        seen += deep
    o_ref[...] = base_ref[...] + adapter_scale * total


def expand(base, low, g, ids, blocks):
    rows = g.shape[0]
    _, rank, width = blocks[0].shape
    tile = min(512, width)
    flat = [block.reshape(-1, width) for block in blocks]
    deep = sum(block.shape[0] for block in flat)
    return pl.pallas_call(
        functools.partial(expand_kernel, rank),
        out_shape=jax.ShapeDtypeStruct((rows, width), jnp.float32),
        grid_spec=pltpu.PrefetchScalarGridSpec(
            num_scalar_prefetch=1,
            grid=(width // tile,),
            in_specs=[
                pl.BlockSpec((rows, 1), lambda i, ids: (0, 0)),
                pl.BlockSpec((rows, 2 * rank), lambda i, ids: (0, 0)),
                pl.BlockSpec((rows, tile), lambda i, ids: (0, i)),
            ]
            + [pl.BlockSpec((block.shape[0], tile), lambda i, ids: (0, i)) for block in flat],
            out_specs=pl.BlockSpec((rows, tile), lambda i, ids: (0, i)),
            scratch_shapes=[pltpu.VMEM((rows, deep), jnp.bfloat16)],
        ),
        compiler_params=pltpu.CompilerParams(vmem_limit_bytes=VMEM),
        cost_estimate=pl.CostEstimate(flops=1, bytes_accessed=1, transcendentals=0),
    )(ids, g, low, base, *flat)


def after(value, *others):
    return lax.optimization_barrier((value, *others))[0]


def wire(total):
    return total.astype(jnp.float16)


def unwire(block):
    return block.astype(jnp.float32)


def by_slots(line, z, weight, tokens):
    width = weight.shape[1] // line

    def sums(target):
        block = lax.dynamic_slice(weight, (0, target * width), (weight.shape[0], width))
        return BASE_WIRE * jnp.dot(tokens, block, preferred_element_type=jnp.float32)

    right = left = 0.0
    for slot in range(1, line):
        ahead, behind = (z - slot) % line, (z + slot) % line
        if 2 * slot <= line:
            one = sums(jnp.where(z < slot, ahead, behind))
            to_right, to_left = one + right, one + left
        else:
            to_right, to_left = sums(ahead) + right, sums(behind) + left
        going_right = [(i, i + 1) for i in range(slot)]
        going_left = [(line - 1 - i, line - 2 - i) for i in range(slot)]
        right = unwire(lax.ppermute(wire(to_right), "tensor", going_right))
        left = unwire(lax.ppermute(wire(to_left), "tensor", going_left))
    return right + left + sums(z)


def on_device(tokens, weight, down_stack, up_stack, fetch_list, choose):
    line = lax.axis_size("tensor")
    owners = lax.axis_size("dp")
    groups = lax.axis_size("groups")
    chips = owners // CORES
    z = lax.axis_index("tensor")
    me = lax.axis_index("dp")
    group = lax.axis_index("groups")
    x, core = me // CORES, me % CORES
    own, rank, width = down_stack.shape
    rows = tokens.shape[0]
    per_owner = fetch_list.shape[2]
    sibling = [(i, i ^ 1) for i in range(owners)]

    def to_sibling(block):
        return lax.ppermute(block, "dp", sibling)

    wanted = (jnp.arange(owners, dtype=jnp.int32)[:, None] * own + fetch_list[0]).reshape(-1)
    picked = choose[:, None] == jnp.arange(owners * per_owner, dtype=jnp.int32)[None, :]
    g = jnp.sum(jnp.where(picked, wanted[None, :], 0), axis=1)

    share = own // groups
    size = share // BANK_PIECES

    def slots(owner, first, count):
        return owner * own + first + jnp.arange(count, dtype=jnp.int32)

    def cross(stack, shift, piece, *gates):
        first = group * share + piece * size
        block = lax.dynamic_slice(stack, (first, 0, 0), (size, rank, width))
        block = lax.ppermute(after(block, *gates), "dp", [(i, (i + shift * CORES) % owners) for i in range(owners)])
        return block, slots((x - shift) % chips * CORES + core, first, size)

    def turn(block, shift, piece):
        found = []
        for step in range(1, groups):
            other = lax.ppermute(block, "groups", [(i, (i + step) % groups) for i in range(groups)])
            first = (group - step) % groups * share + piece * size
            found.append((other, slots((x - shift) % chips * CORES + core, first, size)))
        return found

    def shared(pairs):
        theirs = [(to_sibling(block), ids + jnp.where(core == 0, own, -own)) for block, ids in pairs]
        return pairs + theirs

    def product(target, rows_of):
        block = lax.dynamic_slice(weight, (0, target * width), (weight.shape[0], width))
        return BASE_WIRE * jnp.dot(rows_of, block, preferred_element_type=jnp.float32)

    mine = slots(me, 0, own)

    def shrink_by(tokens, tokens_other, g_both, pairs):
        ids = jnp.concatenate([ids for _, ids in pairs])
        return shrink(tokens, tokens_other, g_both, ids, [block for block, _ in pairs])

    def joined(halves):
        part = halves[:, :rank] + halves[:, rank:]
        part = part[:rows] + to_sibling(part[rows:])
        return jnp.concatenate([part[: rows // 2], part[rows // 2 :]], axis=1)

    def update(base, low, pairs):
        low = jnp.concatenate([low[:, :rank], low[:, rank:]], axis=0)
        ids = jnp.concatenate([ids for _, ids in pairs])
        return expand(base, jnp.concatenate([low, low], axis=1), g[:, None], ids, [block for block, _ in pairs])

    if line != 4 or chips != 2 or groups != 2:
        summed = by_slots(line, z, weight, tokens) * (1.0 / BASE_WIRE)
        g_both = jnp.concatenate([g, to_sibling(g)])[:, None]
        banks = []
        for stack in (down_stack, up_stack):
            pairs = [(stack, mine)]
            for shift in range(1, chips):
                for piece in range(BANK_PIECES):
                    block, ids = cross(stack, shift, piece)
                    pairs += [(block, ids), *turn(block, shift, piece)]
            banks.append(pairs)
        part = joined(shrink_by(tokens, to_sibling(tokens), g_both, banks[0]))
        low = lax.psum(part, "tensor").astype(jnp.bfloat16)
        return update(summed, low, shared(banks[1])).astype(jnp.bfloat16)

    outer = [(0, 1), (3, 2)]
    inner = [(1, 2), (2, 1)]
    both = [(0, 1), (1, 0), (2, 3), (3, 2)]
    low_half = z < 2
    targets = [jnp.where(low_half, 3, 0), jnp.where(low_half, 2, 1), jnp.array([1, 0, 3, 2], jnp.int32)[z]]

    def hop(block, pairs):
        return lax.ppermute(block, "tensor", pairs)

    def part_of(block, span):
        return lax.slice_in_dim(block, span[0], span[0] + span[1])

    spans = [(0, rows // 4), (rows // 4, rows * 3 // 4)]
    d0, d0_ids = cross(down_stack, 1, 0)
    up_other = to_sibling(up_stack)
    first = wire(product(targets[0], tokens))
    first, tokens, g, down, up, up_other = lax.optimization_barrier(
        (first, tokens, g, down_stack, up_stack, up_other)
    )

    a1 = hop(first, outer)
    g_other, tokens_other = to_sibling(g), to_sibling(tokens)
    later = after(tokens, g_other, tokens_other)
    second = wire(product(targets[1], later))
    d0 = after(d0, second)
    d1, d1_ids = cross(down, 1, 1, d0)
    [(d2, d2_ids)] = turn(d0, 1, 0)
    third = wire(product(targets[2], after(later, d0)))
    g_both = jnp.concatenate([g, g_other])[:, None]
    first, second, third, a1, tokens, tokens_other, d1, d2 = lax.optimization_barrier(
        (first, second, third, a1, tokens, tokens_other, d1, d2)
    )

    a2 = hop(second, outer)
    b1 = hop(wire(unwire(first) + unwire(a1)), inner)
    [(d3, d3_ids)] = turn(d1, 1, 1)
    u0, u0_ids = cross(up, 1, 0, d1)
    halves = shrink_by(tokens, tokens_other, g_both, [(down_stack, mine)])
    u0 = after(u0, halves)
    u1, u1_ids = cross(up, 1, 1, u0)
    home = product(z, tokens) * (1.0 / BASE_WIRE)
    later = after(tokens, home)
    halves += shrink_by(later, tokens_other, g_both, [(d0, d0_ids), (d1, d1_ids), (d2, d2_ids), (d3, d3_ids)])
    part = joined(halves)
    [(u2, u2_ids)] = turn(u0, 1, 0)
    ups = [(up, mine), (up_other, slots(me ^ 1, 0, own)), *shared([(u0, u0_ids)])]
    part += hop(after(part, a2), both)
    c1 = [wire(unwire(part_of(third, span)) + unwire(part_of(b1, span))) for span in spans]
    b2 = wire(unwire(second) + unwire(a2))
    part, c1[0], b2, home, *seen = lax.optimization_barrier((part, c1[0], b2, home, *[block for block, _ in ups]))
    ups = [(block, ids) for block, (_, ids) in zip(seen, ups)]

    a3 = [hop(after(block, u2), both) for block in c1]
    part += hop(part, inner)
    b2 = hop(after(b2, part, u2), inner)
    u1 = after(u1, part)
    late = turn(u1, 1, 1)
    low = part.astype(jnp.bfloat16)
    low = jnp.where((z == 1) | (z == 2), low, hop(low, [(1, 0), (2, 3)]))
    u1, u2, low = after(u1, a3[0]), after(u2, a3[0]), after(low, a3[0])
    adapted = update(home, low, ups)
    adapted = update(adapted, low, shared([(u1, u1_ids), (u2, u2_ids)]) + shared(late))
    out = jnp.zeros((rows, width), jnp.bfloat16)
    for arrived, span in zip(a3, spans):
        wired = unwire(arrived) + unwire(part_of(b2, span))
        total = part_of(adapted, span) + wired * (1.0 / BASE_WIRE)
        out = lax.dynamic_update_slice(lax.optimization_barrier(out), total.astype(jnp.bfloat16), (span[0], 0))
    return out


def solution(mesh):
    return jax.shard_map(
        on_device,
        mesh=mesh,
        in_specs=(
            P(("groups", "dp"), "tensor"),
            P("tensor", None),
            P("dp", None, "tensor"),
            P("dp", None, "tensor"),
            P(("groups", "dp"), None, None),
            P(("groups", "dp")),
        ),
        out_specs=P(("groups", "dp"), "tensor"),
        check_vma=False,
    )
```

```python
import functools

import jax
import jax.numpy as jnp
from jax import lax
from jax.experimental import pallas as pl
from jax.experimental.pallas import tpu as pltpu
from jax.sharding import PartitionSpec as P

adapter_scale = 0.5
CORES = 2
BANK_PIECES = 2
BASE_WIRE = 8.0
VMEM = 48 * 1024 * 1024


def ids_of_pair(ids_ref, first, shape, rank):
    lane = lax.broadcasted_iota(jnp.int32, shape, 1)
    return jnp.where(lane < rank, ids_ref[first], ids_ref[first + 1])


def shrink_kernel(rank, steps, ids_ref, g_ref, mine_ref, other_ref, *refs):
    *blocks, o_ref = refs

    def run(tokens_ref):
        tokens = tokens_ref[...]
        g = g_ref[...]
        total = jnp.zeros(o_ref.shape, jnp.float32)
        seen = 0
        for block in blocks:
            part = lax.dot_general(tokens, block[...], (((1,), (1,)), ((), ())), preferred_element_type=jnp.float32)
            for pair in range(block.shape[0] // (2 * rank)):
                ids = ids_of_pair(ids_ref, seen + 2 * pair, o_ref.shape, rank)
                total += jnp.where(g == ids, part[:, pair * 2 * rank : (pair + 1) * 2 * rank], 0.0)
            seen += block.shape[0] // rank
        o_ref[...] = total

    @pl.when(pl.program_id(0) < steps)
    def _():
        run(mine_ref)

    @pl.when(pl.program_id(0) >= steps)
    def _():
        run(other_ref)


def shrink(mine, other, g, ids, blocks):
    rows, width = mine.shape
    rank = blocks[0].shape[1]
    tile = min(256, rows)
    steps = rows // tile
    flat = [block.reshape(-1, width) for block in blocks]
    deep = sum(block.shape[0] for block in flat)
    return pl.pallas_call(
        functools.partial(shrink_kernel, rank, steps),
        out_shape=jax.ShapeDtypeStruct((2 * rows, 2 * rank), jnp.float32),
        grid_spec=pltpu.PrefetchScalarGridSpec(
            num_scalar_prefetch=1,
            grid=(2 * steps,),
            in_specs=[
                pl.BlockSpec((tile, 1), lambda i, ids: (i, 0)),
                pl.BlockSpec((tile, width), lambda i, ids: (jnp.minimum(i, steps - 1), 0)),
                pl.BlockSpec((tile, width), lambda i, ids: (jnp.maximum(i - steps, 0), 0)),
            ]
            + [pl.BlockSpec(block.shape, lambda i, ids: (0, 0)) for block in flat],
            out_specs=pl.BlockSpec((tile, 2 * rank), lambda i, ids: (i, 0)),
        ),
        compiler_params=pltpu.CompilerParams(vmem_limit_bytes=VMEM),
        cost_estimate=pl.CostEstimate(flops=1, bytes_accessed=1, transcendentals=0),
    )(ids, g, mine, other, *flat)


def expand_kernel(rank, ids_ref, g_ref, low_ref, base_ref, *refs):
    *blocks, o_ref, spread_ref = refs

    @pl.when(pl.program_id(0) == 0)
    def _():
        g = g_ref[...]
        low = low_ref[...].astype(jnp.float32)
        for pair in range(spread_ref.shape[1] // (2 * rank)):
            ids = ids_of_pair(ids_ref, 2 * pair, low.shape, rank)
            picked = jnp.where(g == ids, low, 0.0).astype(jnp.bfloat16)
            spread_ref[:, pair * 2 * rank : (pair + 1) * 2 * rank] = picked

    total = jnp.zeros(o_ref.shape, jnp.float32)
    seen = 0
    for block in blocks:
        deep = block.shape[0]
        total += jnp.dot(spread_ref[:, seen : seen + deep], block[...], preferred_element_type=jnp.float32)
        seen += deep
    o_ref[...] = base_ref[...] + adapter_scale * total


def expand(base, low, g, ids, blocks):
    rows = g.shape[0]
    _, rank, width = blocks[0].shape
    tile = min(512, width)
    flat = [block.reshape(-1, width) for block in blocks]
    deep = sum(block.shape[0] for block in flat)
    return pl.pallas_call(
        functools.partial(expand_kernel, rank),
        out_shape=jax.ShapeDtypeStruct((rows, width), jnp.float32),
        grid_spec=pltpu.PrefetchScalarGridSpec(
            num_scalar_prefetch=1,
            grid=(width // tile,),
            in_specs=[
                pl.BlockSpec((rows, 1), lambda i, ids: (0, 0)),
                pl.BlockSpec((rows, 2 * rank), lambda i, ids: (0, 0)),
                pl.BlockSpec((rows, tile), lambda i, ids: (0, i)),
            ]
            + [pl.BlockSpec((block.shape[0], tile), lambda i, ids: (0, i)) for block in flat],
            out_specs=pl.BlockSpec((rows, tile), lambda i, ids: (0, i)),
            scratch_shapes=[pltpu.VMEM((rows, deep), jnp.bfloat16)],
        ),
        compiler_params=pltpu.CompilerParams(vmem_limit_bytes=VMEM),
        cost_estimate=pl.CostEstimate(flops=1, bytes_accessed=1, transcendentals=0),
    )(ids, g, low, base, *flat)


def after(value, *others):
    return lax.optimization_barrier((value, *others))[0]


def wire(total):
    return total.astype(jnp.float16)


def unwire(block):
    return block.astype(jnp.float32)


def by_slots(line, z, weight, tokens):
    width = weight.shape[1] // line

    def sums(target):
        block = lax.dynamic_slice(weight, (0, target * width), (weight.shape[0], width))
        return BASE_WIRE * jnp.dot(tokens, block, preferred_element_type=jnp.float32)

    right = left = 0.0
    for slot in range(1, line):
        ahead, behind = (z - slot) % line, (z + slot) % line
        if 2 * slot <= line:
            one = sums(jnp.where(z < slot, ahead, behind))
            to_right, to_left = one + right, one + left
        else:
            to_right, to_left = sums(ahead) + right, sums(behind) + left
        going_right = [(i, i + 1) for i in range(slot)]
        going_left = [(line - 1 - i, line - 2 - i) for i in range(slot)]
        right = unwire(lax.ppermute(wire(to_right), "tensor", going_right))
        left = unwire(lax.ppermute(wire(to_left), "tensor", going_left))
    return right + left + sums(z)


def on_device(tokens, weight, down_stack, up_stack, fetch_list, choose):
    line = lax.axis_size("tensor")
    owners = lax.axis_size("dp")
    groups = lax.axis_size("groups")
    chips = owners // CORES
    z = lax.axis_index("tensor")
    me = lax.axis_index("dp")
    group = lax.axis_index("groups")
    x, core = me // CORES, me % CORES
    own, rank, width = down_stack.shape
    rows = tokens.shape[0]
    per_owner = fetch_list.shape[2]
    sibling = [(i, i ^ 1) for i in range(owners)]

    def to_sibling(block):
        return lax.ppermute(block, "dp", sibling)

    wanted = (jnp.arange(owners, dtype=jnp.int32)[:, None] * own + fetch_list[0]).reshape(-1)
    picked = choose[:, None] == jnp.arange(owners * per_owner, dtype=jnp.int32)[None, :]
    g = jnp.sum(jnp.where(picked, wanted[None, :], 0), axis=1)

    share = own // groups
    size = share // BANK_PIECES

    def slots(owner, first, count):
        return owner * own + first + jnp.arange(count, dtype=jnp.int32)

    def cross(stack, shift, piece, *gates):
        first = group * share + piece * size
        block = lax.dynamic_slice(stack, (first, 0, 0), (size, rank, width))
        block = lax.ppermute(after(block, *gates), "dp", [(i, (i + shift * CORES) % owners) for i in range(owners)])
        return block, slots((x - shift) % chips * CORES + core, first, size)

    def turn(block, shift, piece):
        found = []
        for step in range(1, groups):
            other = lax.ppermute(block, "groups", [(i, (i + step) % groups) for i in range(groups)])
            first = (group - step) % groups * share + piece * size
            found.append((other, slots((x - shift) % chips * CORES + core, first, size)))
        return found

    def shared(pairs):
        theirs = [(to_sibling(block), ids + jnp.where(core == 0, own, -own)) for block, ids in pairs]
        return pairs + theirs

    def product(target, rows_of):
        block = lax.dynamic_slice(weight, (0, target * width), (weight.shape[0], width))
        return BASE_WIRE * jnp.dot(rows_of, block, preferred_element_type=jnp.float32)

    mine = slots(me, 0, own)

    def shrink_by(tokens, tokens_other, g_both, pairs):
        ids = jnp.concatenate([ids for _, ids in pairs])
        return shrink(tokens, tokens_other, g_both, ids, [block for block, _ in pairs])

    def joined(halves):
        part = halves[:, :rank] + halves[:, rank:]
        part = part[:rows] + to_sibling(part[rows:])
        return jnp.concatenate([part[: rows // 2], part[rows // 2 :]], axis=1)

    def update(base, low, pairs):
        low = jnp.concatenate([low[:, :rank], low[:, rank:]], axis=0)
        ids = jnp.concatenate([ids for _, ids in pairs])
        return expand(base, jnp.concatenate([low, low], axis=1), g[:, None], ids, [block for block, _ in pairs])

    if line != 4 or chips != 2 or groups != 2:
        summed = by_slots(line, z, weight, tokens) * (1.0 / BASE_WIRE)
        g_both = jnp.concatenate([g, to_sibling(g)])[:, None]
        banks = []
        for stack in (down_stack, up_stack):
            pairs = [(stack, mine)]
            for shift in range(1, chips):
                for piece in range(BANK_PIECES):
                    block, ids = cross(stack, shift, piece)
                    pairs += [(block, ids), *turn(block, shift, piece)]
            banks.append(pairs)
        part = joined(shrink_by(tokens, to_sibling(tokens), g_both, banks[0]))
        low = lax.psum(part, "tensor").astype(jnp.bfloat16)
        return update(summed, low, shared(banks[1])).astype(jnp.bfloat16)

    outer = [(0, 1), (3, 2)]
    inner = [(1, 2), (2, 1)]
    both = [(0, 1), (1, 0), (2, 3), (3, 2)]
    low_half = z < 2
    targets = [jnp.where(low_half, 3, 0), jnp.where(low_half, 2, 1), jnp.array([1, 0, 3, 2], jnp.int32)[z]]

    def hop(block, pairs):
        return lax.ppermute(block, "tensor", pairs)

    def part_of(block, span):
        return lax.slice_in_dim(block, span[0], span[0] + span[1])

    spans = [(0, rows // 4), (rows // 4, rows * 3 // 4)]
    d0, d0_ids = cross(down_stack, 1, 0)
    up_other = to_sibling(up_stack)
    first = wire(product(targets[0], tokens))
    first, tokens, g, down, up, up_other = lax.optimization_barrier(
        (first, tokens, g, down_stack, up_stack, up_other)
    )

    a1 = hop(first, outer)
    g_other, tokens_other = to_sibling(g), to_sibling(tokens)
    later = after(tokens, g_other, tokens_other)
    second = wire(product(targets[1], later))
    d0 = after(d0, second)
    d1, d1_ids = cross(down, 1, 1, d0)
    [(d2, d2_ids)] = turn(d0, 1, 0)
    third = wire(product(targets[2], after(later, d0)))
    g_both = jnp.concatenate([g, g_other])[:, None]
    first, second, third, a1, tokens, tokens_other, d1, d2 = lax.optimization_barrier(
        (first, second, third, a1, tokens, tokens_other, d1, d2)
    )

    a2 = hop(second, outer)
    b1 = hop(wire(unwire(first) + unwire(a1)), inner)
    [(d3, d3_ids)] = turn(d1, 1, 1)
    u0, u0_ids = cross(up, 1, 0, d1)
    halves = shrink_by(tokens, tokens_other, g_both, [(down_stack, mine)])
    u0 = after(u0, halves)
    u1, u1_ids = cross(up, 1, 1, u0)
    home = product(z, tokens) * (1.0 / BASE_WIRE)
    later = after(tokens, home)
    halves += shrink_by(later, tokens_other, g_both, [(d0, d0_ids), (d1, d1_ids), (d2, d2_ids), (d3, d3_ids)])
    part = joined(halves)
    [(u2, u2_ids)] = turn(u0, 1, 0)
    ups = [(up, mine), (up_other, slots(me ^ 1, 0, own)), *shared([(u0, u0_ids)])]
    part += hop(after(part, a2), both)
    c1 = [wire(unwire(part_of(third, span)) + unwire(part_of(b1, span))) for span in spans]
    b2 = wire(unwire(second) + unwire(a2))
    part, c1[0], b2, home, *seen = lax.optimization_barrier((part, c1[0], b2, home, *[block for block, _ in ups]))
    ups = [(block, ids) for block, (_, ids) in zip(seen, ups)]

    a3 = [hop(after(block, u2), both) for block in c1]
    part += hop(part, inner)
    b2 = hop(after(b2, part), inner)
    u1 = after(u1, part)
    late = turn(u1, 1, 1)
    low = part.astype(jnp.bfloat16)
    low = jnp.where((z == 1) | (z == 2), low, hop(low, [(1, 0), (2, 3)]))
    u1, u2, low = after(u1, a3[0]), after(u2, a3[0]), after(low, a3[0])
    adapted = update(home, low, ups)
    adapted = update(adapted, low, shared([(u1, u1_ids), (u2, u2_ids)]) + shared(late))
    out = jnp.zeros((rows, width), jnp.bfloat16)
    for arrived, span in zip(a3, spans):
        wired = unwire(arrived) + unwire(part_of(b2, span))
        total = part_of(adapted, span) + wired * (1.0 / BASE_WIRE)
        out = lax.dynamic_update_slice(lax.optimization_barrier(out), total.astype(jnp.bfloat16), (span[0], 0))
    return out


def solution(mesh):
    return jax.shard_map(
        on_device,
        mesh=mesh,
        in_specs=(
            P(("groups", "dp"), "tensor"),
            P("tensor", None),
            P("dp", None, "tensor"),
            P("dp", None, "tensor"),
            P(("groups", "dp"), None, None),
            P(("groups", "dp")),
        ),
        out_specs=P(("groups", "dp"), "tensor"),
        check_vma=False,
    )
```
